32 devices in a mesh: tm: 4 (over y, x), space: 8 (over z, core).
Axes of the slice: x: 2, y: 2, z: 4, core: 2. Of those that a mesh axis runs over, the one named last changes fastest.
Arguments:
- starts: float32 [8, 8, 32, 16, 1024], P('tm', None, 'space'), may hold values from 0 to 2
- pore_mask: int32 [32, 16, 1024], P('space'), may hold values 0 or 1
- phase_label: int32 [32, 16, 1024], P('space'), may hold values from 0 to 3
- diffusivity: float32 [8], replicated, may hold values from 0.08 to 0.16
- stoich: float32 [8], replicated, may hold values from -1 to 1
- phase_rate: float32 [4], replicated, may hold values from 0.02 to 0.1
Outputs:
- ends: float32 [8, 8, 32, 16, 1024], P('tm', None, 'space')
The draws below stay inside these ranges and needn't reach their ends.
Inputs may be any that keep to these rules, and one draw needn't show every extreme that they name: `pore_mask`: 0 marks solid cells, 1 pore cells.
All inputs are finite; a program needn't handle non-finite values. No bound on the sum of `pore_mask` on one device may be relied on, other than what follows from the above.
Results may differ from the reference program's by a relative error of at most 0.00011.
Values sent between devices are 32-bit elements; how exact they have to be, the bound alone decides.
A program may use at most 192 MiB of HBM per device.

```python
import math
import jax
import jax.numpy as jnp
from jax import lax

SPEC = 8
PHASES = 4
SUBSTEPS = 4
NY = 16
NZ = 1024
SLICES = 8
NX = 32


def draw_starts(key, part):
    layer_key, cell_key = jax.random.split(jax.random.fold_in(key, 17))
    layer_high = jax.random.bernoulli(layer_key, 0.5, (NX,))
    spread = jax.random.uniform(cell_key, (SLICES, SPEC, NX, NY, NZ), jnp.float32, 0.0, 1.0)
    width = 0.2
    lower = width * spread
    upper = 2.0 - width * spread
    chosen = jnp.where(layer_high[None, None, :, None, None], upper, lower)
    return chosen.astype(jnp.float32)


def place_ends(values, rng, least, largest):
    spot = [jax.random.randint(jax.random.fold_in(rng, axis), (), 0, length) for axis, length in enumerate(values.shape)]
    main_axis = values.shape.index(max(values.shape))
    neighbour = spot[:main_axis] + [(spot[main_axis] + 1) % values.shape[main_axis]] + spot[main_axis + 1:]
    return values.at[tuple(spot)].set(least).at[tuple(neighbour)].set(largest)


def setup_inputs(seed: int = 0) -> dict:
    keys = jax.random.split(jax.random.key(seed), 7)
    starts = draw_starts(jax.random.fold_in(keys[6], 71), 0)
    pore_mask = place_ends((jax.random.randint(keys[1], (NX, NY, NZ), 0, 4) < 3).astype(jnp.int32), jax.random.fold_in(keys[1], 1), 0, 1)
    phase_label = place_ends(jax.random.randint(keys[2], (NX, NY, NZ), 0, PHASES), jax.random.fold_in(keys[2], 1), 0, PHASES - 1).astype(jnp.int32)
    diffusivity = jnp.clip(jnp.exp(jax.random.uniform(keys[3], (SPEC,), jnp.float32, math.log(0.08), math.log(0.16))), 0.08, 0.16)
    stoich = jnp.clip(jax.random.uniform(keys[4], (SPEC,), jnp.float32, -1.0, 1.0), -1.0, 1.0)
    phase_rate = jnp.clip(jnp.exp(jax.random.uniform(keys[5], (PHASES,), jnp.float32, math.log(0.02), math.log(0.1))), 0.02, 0.1)
    return dict(starts=starts, pore_mask=pore_mask, phase_label=phase_label, diffusivity=diffusivity, stoich=stoich, phase_rate=phase_rate)


def shifted(array, axis, step):
    count = array.shape[axis]
    widths = [(0, 0)] * array.ndim
    if step > 0:
        widths[axis] = (0, step)
        return lax.slice_in_dim(jnp.pad(array, widths), step, step + count, axis=axis)
    widths[axis] = (-step, 0)
    return lax.slice_in_dim(jnp.pad(array, widths), 0, count, axis=axis)


def explicit_step(padded, weight_wide, source, coef, rscale, stoich):
    conc = padded[..., 1:-1, :, :]
    weight = weight_wide[1:-1]
    total = weight_wide[2:] * (padded[..., 2:, :, :] - conc) + weight_wide[:-2] * (padded[..., :-2, :, :] - conc)
    for axis in (1, 2):
        for step in (1, -1):
            total = total + shifted(weight, axis, step) * (shifted(conc, conc.ndim - 3 + axis, step) - conc)
    diffusion = coef[:, None, None, None] * (weight * total)
    rate = source * (1.0 - conc[..., 0, :, :, :] * conc[..., 1, :, :, :])
    return conc + diffusion + rscale * stoich[:, None, None, None] * rate[..., None, :, :, :]


def restrict(array):
    shape = array.shape
    lead = shape[:-3]
    blocks = array.reshape(lead + (shape[-3] // 2, 2, shape[-2] // 2, 2, shape[-1] // 2, 2))
    return jnp.mean(blocks, axis=(-5, -3, -1))


def prolong(array):
    return jnp.repeat(jnp.repeat(jnp.repeat(array, 2, axis=-3), 2, axis=-2), 2, axis=-1)


def wrapped(array):
    return jnp.concatenate([array[..., -1:, :, :], array, array[..., :1, :, :]], axis=-3)


def reference(starts, pore_mask, phase_label, diffusivity, stoich, phase_rate):
    pores = pore_mask.astype(jnp.float32)
    kappa = jnp.zeros(pores.shape, jnp.float32)
    for phase in range(PHASES):
        kappa = kappa + jnp.where(phase_label == phase, phase_rate[phase], jnp.float32(0.0))
    source = pores * kappa
    porosity = restrict(pores)
    coarse_source = restrict(source)
    pores_wide = wrapped(pores)
    porosity_wide = wrapped(porosity)
    coarse_coef = diffusivity * (SUBSTEPS / 4.0)

    def coarse_step(state):
        return explicit_step(wrapped(state), porosity_wide, coarse_source, coarse_coef, float(SUBSTEPS), stoich)

    fines = []
    previous = []
    for slot in range(SLICES):
        state = starts[slot]
        for turn in range(SUBSTEPS):
            state = explicit_step(wrapped(state), pores_wide, source, diffusivity, 1.0, stoich)
        fines.append(state)
        previous.append(coarse_step(restrict(starts[slot])))
    carried = restrict(starts[0])
    results = []
    for slot in range(SLICES):
        advanced = coarse_step(carried)
        finished = prolong(advanced - previous[slot]) + fines[slot]
        results.append(finished)
        carried = restrict(finished)
    return jnp.stack(results)
```

```python
import functools

import jax
import jax.numpy as jnp
from jax import lax
from jax.experimental import pallas as pl
from jax.experimental.pallas import tpu as pltpu
from jax.sharding import PartitionSpec as P

PHASES = 4
SUBSTEPS = 4
HIGHEST = lax.Precision.HIGHEST
VMEM = pl.BlockSpec(memory_space=pltpu.VMEM)
SMEM = pl.BlockSpec(memory_space=pltpu.SMEM)


def call(kernel, outs, specs, args, flops):
    shapes = [jax.ShapeDtypeStruct(shape, jnp.float32) for shape in outs]
    moved = sum(a.size * 4 for a in args) + sum(s.size * 4 for s in shapes)
    return pl.pallas_call(
        kernel,
        out_shape=shapes,
        in_specs=specs,
        out_specs=[VMEM] * len(outs),
        compiler_params=pltpu.CompilerParams(vmem_limit_bytes=48 << 20),
        cost_estimate=pl.CostEstimate(flops=flops, bytes_accessed=moved, transcendentals=0),
    )(*args)


def plane_sum(c):
    rows, lanes = c.shape
    row = lax.broadcasted_iota(jnp.int32, c.shape, 0)
    lane = lax.broadcasted_iota(jnp.int32, c.shape, 1)
    zero = jnp.float32(0.0)
    total = jnp.where(row > 0, pltpu.roll(c, 1, 0), zero)
    total = total + jnp.where(row < rows - 1, pltpu.roll(c, rows - 1, 0), zero)
    total = total + jnp.where(lane > 0, pltpu.roll(c, 1, 1), zero)
    return total + jnp.where(lane < lanes - 1, pltpu.roll(c, lanes - 1, 1), zero)


def kappa_of(label, rate_ref):
    kappa = jnp.zeros(label.shape, jnp.float32)
    for phase in range(PHASES):
        kappa = jnp.where(label == phase, rate_ref[phase], kappa)
    return kappa


def fold(a, rows_out):
    rows, lanes = a.shape
    i = lax.broadcasted_iota(jnp.int32, (rows_out, rows), 0)
    j = lax.broadcasted_iota(jnp.int32, (rows_out, rows), 1)
    left = jnp.where(j // 2 == i, jnp.float32(0.125), jnp.float32(0.0))
    y = jnp.dot(left, a, precision=HIGHEST, preferred_element_type=jnp.float32)
    i = lax.broadcasted_iota(jnp.int32, (256, 128), 0)
    j = lax.broadcasted_iota(jnp.int32, (256, 128), 1)
    right = jnp.where(i // 2 == j, jnp.float32(1.0), jnp.float32(0.0))
    return [
        jnp.dot(y[:, g * 256 : g * 256 + 256], right, precision=HIGHEST, preferred_element_type=jnp.float32)
        for g in range(lanes // 256)
    ]


def spread(a):
    rows, lanes = a.shape
    i = lax.broadcasted_iota(jnp.int32, (2 * rows, rows), 0)
    j = lax.broadcasted_iota(jnp.int32, (2 * rows, rows), 1)
    left = jnp.where(i // 2 == j, jnp.float32(1.0), jnp.float32(0.0))
    y = jnp.dot(left, a, precision=HIGHEST, preferred_element_type=jnp.float32)
    i = lax.broadcasted_iota(jnp.int32, (128, 256), 0)
    j = lax.broadcasted_iota(jnp.int32, (128, 256), 1)
    right = jnp.where(j // 2 == i, jnp.float32(1.0), jnp.float32(0.0))
    return [
        jnp.dot(y[:, g * 128 : g * 128 + 128], right, precision=HIGHEST, preferred_element_type=jnp.float32)
        for g in range(lanes // 128)
    ]


def edge_kernel(starts_ref, mask_ref, *outs):
    tile = mask_ref.shape[0]
    spec = starts_ref.shape[1]
    for side, layer in ((0, 0), (1, tile - 1)):
        w = mask_ref[layer].astype(jnp.float32)
        outs[4 + side][0] = w
        for which in range(2):
            for k in range(spec):
                outs[2 * which + side][k, 0] = starts_ref[which, k, layer] * w


def coarse_fields_kernel(mask_ref, label_ref, rate_ref, por_ref, src_ref):
    tile, ny, nz = mask_ref.shape
    pores = mask_ref[...].astype(jnp.float32)
    source = pores * kappa_of(label_ref[...], rate_ref)
    for value, out in ((pores, por_ref), (source, src_ref)):
        pair = value.reshape(tile // 2, 2, ny, nz)
        pair = (pair[:, 0] + pair[:, 1]).reshape(tile // 2 * ny, nz)
        for g, part in enumerate(fold(pair, pair.shape[0] // 2)):
            out[:, :, g * 128 : g * 128 + 128] = part.reshape(tile // 2, ny // 2, 128)


def restrict_kernel(which, merge, *refs):
    if merge:
        starts_ref, mask_ref, u_ref, prev_ref, out_ref = refs
    else:
        starts_ref, out_ref = refs
    _, spec, tile, ny, nz = starts_ref.shape

    def layer(k, i):
        if merge:
            return jnp.where(mask_ref[i] != 0, u_ref[k, i], starts_ref[which, k, i])
        return starts_ref[which, k, i]

    for k in range(spec):
        pair = jnp.concatenate(
            [layer(k, 2 * i) + layer(k, 2 * i + 1) for i in range(tile // 2)], axis=0
        )
        for g, part in enumerate(fold(pair, pair.shape[0] // 2)):
            part = part.reshape(tile // 2, ny // 2, 128)
            lanes = slice(g * 128, g * 128 + 128)
            if merge:
                part = part - prev_ref[k, :, :, lanes]
            out_ref[k, :, :, lanes] = part


def fine_kernel(
    first, u_ref, lo_ref, hi_ref, mask_ref, wlo_ref, whi_ref, label_ref,
    rate_ref, d_ref, st_ref, out_ref, elo_ref, ehi_ref, w_s, wide_s, src_s,
):
    tile = mask_ref.shape[0]
    spec = out_ref.shape[0]

    def cell(k, i):
        if i < 0:
            return lo_ref[k, 0]
        if i >= tile:
            return hi_ref[k, 0]
        if first is not None:
            return u_ref[first, k, i] * w_s[i]
        return u_ref[k, i]

    for i in range(tile):
        w_s[i] = mask_ref[i].astype(jnp.float32)
    for i in range(tile):
        below = w_s[i - 1] if i else wlo_ref[0]
        above = w_s[i + 1] if i + 1 < tile else whi_ref[0]
        wide_s[i] = w_s[i] * (plane_sum(w_s[i]) + below + above)
        source = w_s[i] * kappa_of(label_ref[i], rate_ref)
        src_s[i] = source * (1.0 - cell(0, i) * cell(1, i))

    def body(k, carry):
        d = d_ref[k]
        st = st_ref[k]
        for i in range(tile):
            c = cell(k, i)
            total = plane_sum(c) + cell(k, i - 1) + cell(k, i + 1)
            new = c + d * (w_s[i] * total - wide_s[i] * c) + st * src_s[i]
            out_ref[k, i] = new
            if i == 0:
                elo_ref[k, 0] = new
            if i == tile - 1:
                ehi_ref[k, 0] = new
        return carry

    lax.fori_loop(0, spec, body, 0)


def coarse_step(cell, por, src, d_ref, st_ref, spec, layers, emit):
    for i in layers:
        p = por(i)
        wide = p * (plane_sum(p) + por(i - 1) + por(i + 1))
        below, above = por(i - 1), por(i + 1)
        rate = float(SUBSTEPS) * (src(i) * (1.0 - cell(0, i) * cell(1, i)))
        for k in range(spec):
            c = cell(k, i)
            total = plane_sum(p * c) + below * cell(k, i - 1) + above * cell(k, i + 1)
            emit(k, i, c + d_ref[k] * (p * total - wide * c) + st_ref[k] * rate)


def section_kernel(
    lo, own, hi, q1lo, q1, q1hi, q2, prev1, prev2, plo, p, phi, slo, s, shi,
    d_ref, st_ref, next_ref, d1_ref, d2_ref, mid,
):
    spec = own.shape[0]

    def tri(a, b, c, n):
        return lambda i: a[i + n] if i < 0 else (b[i] if i < 2 else c[i - 2])

    def tri_k(a, b, c, n):
        return lambda k, i: a[k, i + n] if i < 0 else (b[k, i] if i < 2 else c[k, i - 2])

    por = tri(plo, p, phi, 2)
    src = tri(slo, s, shi, 1)
    q = tri_k(q1lo, q1, q1hi, 1)

    def first(k, i, g):
        mid[k, i + 1] = g + q(k, i)
        if 0 <= i < 2:
            d1_ref[k, i] = g - prev1[k, i]

    coarse_step(tri_k(lo, own, hi, 2), por, src, d_ref, st_ref, spec, (-1, 0, 1, 2), first)

    def second(k, i, g):
        next_ref[k, i] = g + q2[k, i]
        d2_ref[k, i] = g - prev2[k, i]

    coarse_step(lambda k, i: mid[k, i + 1], por, src, d_ref, st_ref, spec, (0, 1), second)


def prev_kernel(lo, own, hi, plo, p, phi, s, d_ref, st_ref, out_ref):
    spec = own.shape[0]
    last = lo.shape[1]

    def cell(k, i):
        return lo[k, last - 1] if i < 0 else (own[k, i] if i < 2 else hi[k, 0])

    def por(i):
        return plo[1] if i < 0 else (p[i] if i < 2 else phi[0])

    def emit(k, i, g):
        out_ref[k, i] = g

    coarse_step(cell, por, lambda i: s[i], d_ref, st_ref, spec, (0, 1), emit)


def final_kernel(starts_ref, mask_ref, ua_ref, ub_ref, da_ref, db_ref, out_ref):
    _, tile, ny, nz = starts_ref.shape
    _, half, cy, cz = da_ref.shape
    which = pl.program_id(0)

    def write(u_ref, delta_ref):
        for g, part in enumerate(spread(delta_ref[0].reshape(half * cy, cz))):
            part = part.reshape(half, ny, 256)
            lanes = slice(g * 256, g * 256 + 256)
            for i in range(tile):
                fine = jnp.where(mask_ref[i, :, lanes] != 0, u_ref[0, i, :, lanes], starts_ref[0, i, :, lanes])
                out_ref[0, i, :, lanes] = part[i // 2] + fine

    @pl.when(which == 0)
    def _():
        write(ua_ref, da_ref)

    @pl.when(which == 1)
    def _():
        write(ub_ref, db_ref)


def final(starts, mask, ua, ub, da, db):
    count, spec, tile, ny, nz = starts.shape
    a = lambda n, k: (jnp.where(n == 0, k, spec - 1), 0, 0, 0)
    b = lambda n, k: (jnp.where(n == 0, 0, k), 0, 0, 0)
    fine = (1, tile, ny, nz)
    coarse = (1,) + da.shape[1:]
    return pl.pallas_call(
        final_kernel,
        grid=(count, spec),
        out_shape=jax.ShapeDtypeStruct(starts.shape, jnp.float32),
        in_specs=[
            pl.BlockSpec((None,) + fine, lambda n, k: (n, k, 0, 0, 0)),
            pl.BlockSpec((tile, ny, nz), lambda n, k: (0, 0, 0)),
            pl.BlockSpec(fine, a),
            pl.BlockSpec(fine, b),
            pl.BlockSpec(coarse, a),
            pl.BlockSpec(coarse, b),
        ],
        out_specs=pl.BlockSpec((None,) + fine, lambda n, k: (n, k, 0, 0, 0)),
        cost_estimate=pl.CostEstimate(flops=4 * starts.size, bytes_accessed=12 * starts.size, transcendentals=0),
    )(starts, mask, ua, ub, da, db)


def around(low_part, high_part):
    count = lax.axis_size("space")
    up = [(i, (i + 1) % count) for i in range(count)]
    down = [(target, source) for source, target in up]
    return lax.ppermute(high_part, "space", up), lax.ppermute(low_part, "space", down)


def local(starts, mask, label, diffusivity, stoich, rate):
    _, spec, tile, ny, nz = starts.shape
    edge = (spec, 1, ny, nz)
    state = (spec, tile, ny, nz)
    coarse = (spec, tile // 2, ny // 2, nz // 2)
    plane = (tile // 2, ny // 2, nz // 2)

    ea_lo, ea_hi, eb_lo, eb_hi, w_lo, w_hi = call(
        edge_kernel, [edge] * 4 + [(1, ny, nz)] * 2, [VMEM] * 2, (starts, mask), 1 << 20
    )
    wb, wa = around(w_lo, w_hi)
    halo = [around(ea_lo, ea_hi), around(eb_lo, eb_hi)]
    por, src = call(
        coarse_fields_kernel, [plane] * 2, [VMEM, VMEM, SMEM], (mask, label, rate), 1 << 26
    )
    pb, pa = around(por, por)
    sb, sa = around(src[:1], src[1:])
    rs = [
        call(functools.partial(restrict_kernel, n, False), [coarse], [VMEM], (starts,), 1 << 28)[0]
        for n in range(2)
    ]
    v_lo, v_hi = around(rs[0], rs[0])
    r_lo, r_hi = around(rs[1][:, :1], rs[1][:, 1:])

    def previous(lo, own, hi):
        return call(
            prev_kernel, [coarse], [VMEM] * 7 + [SMEM] * 2,
            (lo, own, hi, pb, por, pa, src, diffusivity, stoich), 1 << 22,
        )[0]

    states = [starts, starts]
    prev = [None, None]
    for turn in range(SUBSTEPS):
        for n in range(2):
            below, above = halo[n]
            args = (states[n], below, above, mask, wb, wa, label, rate, diffusivity, stoich)
            first = n if turn == 0 else None
            shapes = [jax.ShapeDtypeStruct(x, jnp.float32) for x in (state, edge, edge)]
            states[n], e_lo, e_hi = pl.pallas_call(
                functools.partial(fine_kernel, first),
                out_shape=shapes,
                in_specs=[VMEM] * 7 + [SMEM] * 3,
                out_specs=[VMEM] * 3,
                scratch_shapes=[pltpu.VMEM((tile, ny, nz), jnp.float32)] * 3,
                compiler_params=pltpu.CompilerParams(vmem_limit_bytes=32 << 20),
                cost_estimate=pl.CostEstimate(flops=1 << 24, bytes_accessed=6 << 20, transcendentals=0),
            )(*args)
            if turn + 1 < SUBSTEPS:
                halo[n] = around(e_lo, e_hi)
    prev[0] = previous(v_lo, rs[0], v_hi)
    prev[1] = previous(r_lo, rs[1], r_hi)
    q = [
        call(
            functools.partial(restrict_kernel, n, True), [coarse], [VMEM] * 4,
            (starts, mask, states[n], prev[n]), 1 << 28,
        )[0]
        for n in range(2)
    ]
    q_lo, q_hi = around(q[0][:, :1], q[0][:, 1:])

    def section(lo, own, hi):
        return pl.pallas_call(
            section_kernel,
            out_shape=[jax.ShapeDtypeStruct(coarse, jnp.float32)] * 3,
            in_specs=[VMEM] * 15 + [SMEM] * 2,
            out_specs=[VMEM] * 3,
            scratch_shapes=[pltpu.VMEM((spec, tile // 2 + 2) + coarse[2:], jnp.float32)],
            cost_estimate=pl.CostEstimate(flops=1 << 22, bytes_accessed=2 << 20, transcendentals=0),
        )(lo, own, hi, q_lo, q[0], q_hi, q[1], prev[0], prev[1], pb, por, pa, sb, src, sa, diffusivity, stoich)

    place = lax.axis_index("tm")
    sections = lax.axis_size("tm")
    count = lax.axis_size("space")
    current = [jnp.where(place == 0, x, 0.0) for x in (v_lo, rs[0], v_hi)]
    for target in range(1, sections):
        out = section(*current)[0]
        base, there = (target - 1) * count, target * count
        for slot, step in ((0, 1), (1, 0), (2, -1)):
            pairs = [(base + i, there + (i + step) % count) for i in range(count)]
            current[slot] = current[slot] + lax.ppermute(out, ("tm", "space"), pairs)
    _, delta_a, delta_b = section(*current)
    return final(starts, mask, states[0], states[1], delta_a, delta_b)


def solution(mesh):
    placed = (
        P("tm", None, "space", None, None),
        P("space", None, None),
        P("space", None, None),
        P(),
        P(),
        P(),
    )
    return jax.shard_map(
        local,
        mesh=mesh,
        in_specs=placed,
        out_specs=P("tm", None, "space", None, None),
        check_vma=False,
    )
```

```python
import functools

import jax
import jax.numpy as jnp
from jax import lax
from jax.experimental import pallas as pl
from jax.experimental.pallas import tpu as pltpu
from jax.sharding import PartitionSpec as P

PHASES = 4
SUBSTEPS = 4
VMEM = pl.BlockSpec(memory_space=pltpu.VMEM)
SMEM = pl.BlockSpec(memory_space=pltpu.SMEM)


def call(kernel, outs, specs, args, flops):
    shapes = [jax.ShapeDtypeStruct(shape, jnp.float32) for shape in outs]
    moved = sum(a.size * 4 for a in args) + sum(s.size * 4 for s in shapes)
    return pl.pallas_call(
        kernel,
        out_shape=shapes,
        in_specs=specs,
        out_specs=[VMEM] * len(outs),
        compiler_params=pltpu.CompilerParams(vmem_limit_bytes=48 << 20),
        cost_estimate=pl.CostEstimate(flops=flops, bytes_accessed=moved, transcendentals=0),
    )(*args)


def plane_sum(c):
    rows, lanes = c.shape
    row = lax.broadcasted_iota(jnp.int32, c.shape, 0)
    lane = lax.broadcasted_iota(jnp.int32, c.shape, 1)
    zero = jnp.float32(0.0)
    total = jnp.where(row > 0, pltpu.roll(c, 1, 0), zero)
    total = total + jnp.where(row < rows - 1, pltpu.roll(c, rows - 1, 0), zero)
    total = total + jnp.where(lane > 0, pltpu.roll(c, 1, 1), zero)
    return total + jnp.where(lane < lanes - 1, pltpu.roll(c, lanes - 1, 1), zero)


def kappa_of(label, rate_ref):
    kappa = jnp.zeros(label.shape, jnp.float32)
    for phase in range(PHASES):
        kappa = jnp.where(label == phase, rate_ref[phase], kappa)
    return kappa


def pieces(a):
    high = a.astype(jnp.bfloat16)
    rest = a - high.astype(jnp.float32)
    middle = rest.astype(jnp.bfloat16)
    low = (rest - middle.astype(jnp.float32)).astype(jnp.bfloat16)
    return low, middle, high


def table(shape, value):
    i = lax.broadcasted_iota(jnp.int32, shape, 0)
    j = lax.broadcasted_iota(jnp.int32, shape, 1)
    same = (i // 2 == j) if shape[0] > shape[1] else (j // 2 == i)
    return jnp.where(same, jnp.float32(value), jnp.float32(0.0)).astype(jnp.bfloat16)


def times(a, right):
    return sum(jnp.dot(x, right, preferred_element_type=jnp.float32) for x in pieces(a))


def from_left(left, a):
    return sum(jnp.dot(left, x, preferred_element_type=jnp.float32) for x in pieces(a))


def fold(a):
    rows, lanes = a.shape
    left = table((rows // 2, rows), 0.125)
    right = table((256, 128), 1.0)
    return [from_left(left, times(a[:, g * 256 : g * 256 + 256], right)) for g in range(lanes // 256)]


def spread(a):
    rows, lanes = a.shape
    y = from_left(table((2 * rows, rows), 1.0), a)
    right = table((128, 256), 1.0)
    return [times(y[:, g * 128 : g * 128 + 128], right) for g in range(lanes // 128)]


def edge_kernel(starts_ref, mask_ref, *outs):
    tile = mask_ref.shape[0]
    spec = starts_ref.shape[1]
    for side, layer in ((0, 0), (1, tile - 1)):
        w = mask_ref[layer].astype(jnp.float32)
        outs[side][spec, 0] = w
        for which in range(2):
            for k in range(spec):
                outs[2 * which + side][k, 0] = starts_ref[which, k, layer] * w


def coarse_fields_kernel(mask_ref, label_ref, rate_ref, out_ref):
    tile, ny, nz = mask_ref.shape
    half = tile // 2
    pores = mask_ref[...].astype(jnp.float32)
    source = pores * kappa_of(label_ref[...], rate_ref)
    for n, value in enumerate((pores, source)):
        pair = value.reshape(half, 2, ny, nz)
        pair = (pair[:, 0] + pair[:, 1]).reshape(half * ny, nz)
        for g, part in enumerate(fold(pair)):
            out_ref[n * half : n * half + half, :, g * 128 : g * 128 + 128] = part.reshape(half, ny // 2, 128)


def fold_all(layer, spec, tile, ny, nz):
    pair = [layer(k, 2 * i) + layer(k, 2 * i + 1) for k in range(spec) for i in range(tile // 2)]
    for g, part in enumerate(fold(jnp.concatenate(pair, axis=0))):
        yield slice(g * 128, g * 128 + 128), part.reshape(spec, tile // 2, ny // 2, 128)


def restrict_starts_kernel(starts_ref, out_ref, elo_ref, ehi_ref):
    count, spec, tile, ny, nz = starts_ref.shape
    for n in range(count):
        for lanes, part in fold_all(lambda k, i: starts_ref[n, k, i], spec, tile, ny, nz):
            out_ref[n, :, :, :, lanes] = part
            elo_ref[n, :, :, :, lanes] = part[:, :1]
            ehi_ref[n, :, :, :, lanes] = part[:, -1:]


def advance_kernel(which, starts_ref, mask_ref, u_ref, prev_ref, out_ref, *edges):
    _, spec, tile, ny, nz = starts_ref.shape

    def layer(k, i):
        return jnp.where(mask_ref[i] != 0, u_ref[k, i], starts_ref[which, k, i])

    for lanes, part in fold_all(layer, spec, tile, ny, nz):
        part = part - prev_ref[:, :, :, lanes]
        out_ref[:, :, :, lanes] = part
        if edges:
            edges[0][:, :, :, lanes] = part[:, :1]
            edges[1][:, :, :, lanes] = part[:, -1:]


def fine_kernel(
    first, u_ref, lo_ref, hi_ref, mask_ref, wlo_ref, whi_ref, label_ref,
    rate_ref, d_ref, st_ref, out_ref, elo_ref, ehi_ref, w_s, wide_s, src_s,
):
    tile = mask_ref.shape[0]
    spec = out_ref.shape[0]

    def cell(k, i):
        if i < 0:
            return lo_ref[k, 0]
        if i >= tile:
            return hi_ref[k, 0]
        if first is not None:
            return u_ref[first, k, i] * w_s[i]
        return u_ref[k, i]

    for i in range(tile):
        w_s[i] = mask_ref[i].astype(jnp.float32)
    for i in range(tile):
        below = w_s[i - 1] if i else wlo_ref[spec, 0]
        above = w_s[i + 1] if i + 1 < tile else whi_ref[spec, 0]
        wide_s[i] = w_s[i] * (plane_sum(w_s[i]) + below + above)
        source = w_s[i] * kappa_of(label_ref[i], rate_ref)
        src_s[i] = source * (1.0 - cell(0, i) * cell(1, i))

    def body(k, carry):
        d = d_ref[k]
        st = st_ref[k]
        for i in range(tile):
            c = cell(k, i)
            total = plane_sum(c) + cell(k, i - 1) + cell(k, i + 1)
            new = c + d * (w_s[i] * total - wide_s[i] * c) + st * src_s[i]
            out_ref[k, i] = new
            if i == 0:
                elo_ref[k, 0] = new
            if i == tile - 1:
                ehi_ref[k, 0] = new
        return carry

    lax.fori_loop(0, spec, body, 0)


def coarse_step(cell, por, src, d_ref, st_ref, spec, layers, emit):
    for i in layers:
        p = por(i)
        wide = p * (plane_sum(p) + por(i - 1) + por(i + 1))
        below, above = por(i - 1), por(i + 1)
        rate = float(SUBSTEPS) * (src(i) * (1.0 - cell(0, i) * cell(1, i)))
        for k in range(spec):
            c = cell(k, i)
            total = plane_sum(p * c) + below * cell(k, i - 1) + above * cell(k, i + 1)
            emit(k, i, c + d_ref[k] * (p * total - wide * c) + st_ref[k] * rate)


def section_kernel(
    received, q1lo, q1, q1hi, q2, prev1, prev2, flo, f, fhi, gate_ref, d_ref, st_ref, *refs
):
    parts = refs[: 3 * received]
    next_ref, d1_ref, d2_ref, start, mid = refs[3 * received :]
    spec = q1.shape[0]
    for side in range(3):
        value = jnp.zeros(q1.shape, jnp.float32)
        for part in parts[side::3]:
            value = value + part[...]
        start[:, 2 * side : 2 * side + 2] = value
    gate = gate_ref[0]

    def por(i):
        return flo[i + 2] if i < 0 else (f[i] if i < 2 else fhi[i - 2])

    def src(i):
        return flo[i + 4] if i < 0 else (f[i + 2] if i < 2 else fhi[i])

    def q(k, i):
        return q1lo[k, 0] if i < 0 else (q1[k, i] if i < 2 else q1hi[k, 0])

    def first(k, i, g):
        g = gate * g
        mid[k, i + 1] = g + q(k, i)
        if 0 <= i < 2:
            d1_ref[k, i] = g - prev1[k, i]

    coarse_step(lambda k, i: start[k, i + 2], por, src, d_ref, st_ref, spec, (-1, 0, 1, 2), first)

    def second(k, i, g):
        next_ref[k, i] = g + q2[k, i]
        d2_ref[k, i] = g - prev2[k, i]

    coarse_step(lambda k, i: mid[k, i + 1], por, src, d_ref, st_ref, spec, (0, 1), second)


def prev_kernel(lo, own, hi, flo, f, fhi, gate_ref, d_ref, st_ref, *outs):
    spec = own.shape[1]

    def por(i):
        return flo[1] if i < 0 else (f[i] if i < 2 else fhi[0])

    for n, out_ref in enumerate(outs):

        def cell(k, i):
            return lo[n, k, 0] if i < 0 else (own[n, k, i] if i < 2 else hi[n, k, 0])

        def emit(k, i, g):
            out_ref[k, i] = gate_ref[0] * g if n == 0 else g

        coarse_step(cell, por, lambda i: f[i + 2], d_ref, st_ref, spec, (0, 1), emit)


def final_kernel(starts_ref, mask_ref, ua_ref, ub_ref, da_ref, db_ref, out_ref):
    _, tile, ny, nz = starts_ref.shape
    spec, half, cy, cz = da_ref.shape
    which = pl.program_id(0)

    def write(u_ref, delta_ref):
        for g, part in enumerate(spread(delta_ref[...].reshape(spec * half * cy, cz))):
            part = part.reshape(spec, half, ny, 256)
            lanes = slice(g * 256, g * 256 + 256)
            for i in range(tile):
                keep = (mask_ref[i, :, lanes] != 0)[None]
                fine = jnp.where(keep, u_ref[:, i, :, lanes], starts_ref[:, i, :, lanes])
                out_ref[:, i, :, lanes] = part[:, i // 2] + fine

    @pl.when(which == 0)
    def _():
        write(ua_ref, da_ref)

    @pl.when(which == 1)
    def _():
        write(ub_ref, db_ref)


def final(starts, mask, ua, ub, da, db):
    count, spec, tile, ny, nz = starts.shape
    a = lambda n, k: (jnp.where(n == 0, k, 1), 0, 0, 0)
    b = lambda n, k: (jnp.where(n == 0, 0, k), 0, 0, 0)
    fine = (spec // 2, tile, ny, nz)
    coarse = (spec // 2,) + da.shape[1:]
    return pl.pallas_call(
        final_kernel,
        grid=(count, 2),
        out_shape=jax.ShapeDtypeStruct(starts.shape, jnp.float32),
        in_specs=[
            pl.BlockSpec((None,) + fine, lambda n, k: (n, k, 0, 0, 0)),
            pl.BlockSpec((tile, ny, nz), lambda n, k: (0, 0, 0)),
            pl.BlockSpec(fine, a),
            pl.BlockSpec(fine, b),
            pl.BlockSpec(coarse, a),
            pl.BlockSpec(coarse, b),
        ],
        out_specs=pl.BlockSpec((None,) + fine, lambda n, k: (n, k, 0, 0, 0)),
        compiler_params=pltpu.CompilerParams(vmem_limit_bytes=32 << 20),
        cost_estimate=pl.CostEstimate(flops=4 * starts.size, bytes_accessed=12 * starts.size, transcendentals=0),
    )(starts, mask, ua, ub, da, db)


def around(low_part, high_part):
    count = lax.axis_size("space")
    up = [(i, (i + 1) % count) for i in range(count)]
    down = [(target, source) for source, target in up]
    return lax.ppermute(high_part, "space", up), lax.ppermute(low_part, "space", down)


def local(starts, mask, label, diffusivity, stoich, rate):
    _, spec, tile, ny, nz = starts.shape
    edge = (spec, 1, ny, nz)
    edge_more = (spec + 1, 1, ny, nz)
    state = (spec, tile, ny, nz)
    coarse = (spec, tile // 2, ny // 2, nz // 2)
    coarse_edge = (spec, 1) + coarse[2:]
    place = lax.axis_index("tm")
    gate = jnp.where(place == 0, 0.0, 1.0).astype(jnp.float32).reshape(1)

    ea_lo, ea_hi, eb_lo, eb_hi = call(
        edge_kernel, [edge_more] * 2 + [edge] * 2, [VMEM] * 2, (starts, mask), 1 << 20
    )
    halo = [around(ea_lo, ea_hi), around(eb_lo, eb_hi)]
    wb, wa = halo[0]
    fields = call(
        coarse_fields_kernel, [(tile,) + coarse[2:]], [VMEM, VMEM, SMEM], (mask, label, rate), 1 << 26
    )[0]
    f_lo, f_hi = around(fields, fields)
    rs, r_lo, r_hi = call(
        restrict_starts_kernel, [(2,) + coarse] + [(2,) + coarse_edge] * 2, [VMEM], (starts,), 1 << 29
    )
    r_lo, r_hi = around(r_lo, r_hi)

    states = [starts, starts]
    for turn in range(SUBSTEPS):
        for n in range(2):
            below, above = halo[n]
            args = (states[n], below, above, mask, wb, wa, label, rate, diffusivity, stoich)
            first = n if turn == 0 else None
            shapes = [jax.ShapeDtypeStruct(x, jnp.float32) for x in (state, edge, edge)]
            states[n], e_lo, e_hi = pl.pallas_call(
                functools.partial(fine_kernel, first),
                out_shape=shapes,
                in_specs=[VMEM] * 7 + [SMEM] * 3,
                out_specs=[VMEM] * 3,
                scratch_shapes=[pltpu.VMEM((tile, ny, nz), jnp.float32)] * 3,
                compiler_params=pltpu.CompilerParams(vmem_limit_bytes=32 << 20),
                cost_estimate=pl.CostEstimate(flops=1 << 24, bytes_accessed=6 << 20, transcendentals=0),
            )(*args)
            if turn + 1 < SUBSTEPS:
                halo[n] = around(e_lo, e_hi)
    prev = call(
        prev_kernel, [coarse] * 2, [VMEM] * 6 + [SMEM] * 3,
        (r_lo, rs, r_hi, f_lo, fields, f_hi, gate, diffusivity, stoich), 1 << 23,
    )
    q1, q_lo, q_hi = call(
        functools.partial(advance_kernel, 0), [coarse] + [coarse_edge] * 2, [VMEM] * 4,
        (starts, mask, states[0], prev[0]), 1 << 28,
    )
    q_lo, q_hi = around(q_lo, q_hi)
    q2 = call(
        functools.partial(advance_kernel, 1), [coarse], [VMEM] * 4,
        (starts, mask, states[1], prev[1]), 1 << 28,
    )[0]

    def section(parts):
        return pl.pallas_call(
            functools.partial(section_kernel, len(parts) // 3),
            out_shape=[jax.ShapeDtypeStruct(coarse, jnp.float32)] * 3,
            in_specs=[VMEM] * 9 + [SMEM] * 3 + [VMEM] * len(parts),
            out_specs=[VMEM] * 3,
            scratch_shapes=[
                pltpu.VMEM((spec, 6) + coarse[2:], jnp.float32),
                pltpu.VMEM((spec, 4) + coarse[2:], jnp.float32),
            ],
            compiler_params=pltpu.CompilerParams(vmem_limit_bytes=32 << 20),
            cost_estimate=pl.CostEstimate(flops=1 << 22, bytes_accessed=2 << 20, transcendentals=0),
        )(q_lo, q1, q_hi, q2, prev[0], prev[1], f_lo, fields, f_hi, gate, diffusivity, stoich, *parts)

    sections = lax.axis_size("tm")
    count = lax.axis_size("space")
    parts = []
    for target in range(1, sections):
        out = section(parts)[0]
        base, there = (target - 1) * count, target * count
        for step in (1, 0, -1):
            pairs = [(base + i, there + (i + step) % count) for i in range(count)]
            parts.append(lax.ppermute(out, ("tm", "space"), pairs))
    _, delta_a, delta_b = section(parts)
    return final(starts, mask, states[0], states[1], delta_a, delta_b)


def solution(mesh):
    placed = (
        P("tm", None, "space", None, None),
        P("space", None, None),
        P("space", None, None),
        P(),
        P(),
        P(),
    )
    return jax.shard_map(
        local,
        mesh=mesh,
        in_specs=placed,
        out_specs=P("tm", None, "space", None, None),
        check_vma=False,
    )
```
